128 devices in a mesh: client: 4 (over x), row: 4 (over z_lo, core), col: 8 (over y, z_hi).
Axes of the slice: x: 4, y: 4, z: 4 (z_hi: 2, z_lo: 2; z = z_hi * 2 + z_lo), core: 2. Of those that a mesh axis runs over, the one named last changes fastest.
Arguments:
- frozen_up_weight: bfloat16 [2, 8192, 28672], P(None, 'client', ('row', 'col')), may hold values from -3 to 3
- adapter_down_stack: bfloat16 [2, 256, 8192], P(None, ('row', 'col'), 'client'), may hold values from -6 to 6
- adapter_up_stack: bfloat16 [2, 256, 28672], P(None, 'client', ('row', 'col')), may hold values from -0.375 to 0.375
- participant_weight: float32 [16], replicated, may hold values from 0.25 to 1
Outputs:
- merged: bfloat16 [2, 8192, 28672], P(None, ('client', 'row', 'col'))
The draws below stay inside these ranges and needn't reach their ends.
All inputs are finite; a program needn't handle non-finite values.
Results may differ from the reference program's by a relative error of at most 0.0042.
Values may be sent and summed in bfloat16 or wider, within the bound.
No kernel may reach another device: no remote copies, remote signals or barrier semaphores. Data moves between devices by JAX's collectives and lax.ppermute only.
A program may use at most 128 MiB of HBM per device.

```python
import math
import jax
import jax.numpy as jnp
from jax import lax

MODEL_WIDTH = 8192
HIDDEN_WIDTH = 28672
RANK = 16
CLIENTS = 16
MERGED_LAYERS = 2
STACKED_RANK = 256


def level_of(own_key, extent, split, least, largest):
    gain = 1.0
    for dim, blocks in split:
        heights = jax.random.uniform(jax.random.fold_in(jax.random.fold_in(own_key, 6), dim), (blocks,), jnp.float32, least / len(split), largest / len(split))
        gain = gain * jnp.repeat(jnp.exp(heights), extent[dim] // blocks).reshape((-1,) + (1,) * (len(extent) - 1 - dim))
    return gain


def normal_values(rng, extent, deviation, bound, split=(), kind=jnp.bfloat16):
    result = deviation * jax.random.normal(rng, extent, jnp.float32)
    if split:
        result = result * level_of(rng, extent, split, -0.22, 0.18)
    return jnp.clip(result, -bound, bound).astype(kind)


def setup_inputs(seed: int = 0) -> dict:
    key_of = jax.random.split(jax.random.key(seed), 5)
    frozen_up_weight = normal_values(key_of[0], (MERGED_LAYERS, MODEL_WIDTH, HIDDEN_WIDTH), 0.5, 3.0, ((1, 4), (2, 32)))
    adapter_down_stack = normal_values(key_of[1], (MERGED_LAYERS, STACKED_RANK, MODEL_WIDTH), 1.0, 6.0, ((1, 32), (2, 4)))
    adapter_up_stack = normal_values(key_of[2], (MERGED_LAYERS, STACKED_RANK, HIDDEN_WIDTH), 0.0625, 0.375, ((1, 4), (2, 32)))
    participant_weight = jnp.clip(jnp.exp(jax.random.uniform(key_of[3], (CLIENTS,), jnp.float32, math.log(0.25), math.log(1.0))), 0.25, 1.0)
    return dict(frozen_up_weight=frozen_up_weight, adapter_down_stack=adapter_down_stack, adapter_up_stack=adapter_up_stack, participant_weight=participant_weight)


def reference(frozen_up_weight, adapter_down_stack, adapter_up_stack, participant_weight):
    owners = jnp.arange(STACKED_RANK, dtype=jnp.int32) // RANK
    adapter_scale = participant_weight[owners]
    block = min(MODEL_WIDTH, 512)
    count = MODEL_WIDTH // block
    results = []
    for layer_index in range(MERGED_LAYERS):
        scaled_update = (adapter_scale[:, None] * adapter_down_stack[layer_index].astype(jnp.float32)).astype(jnp.bfloat16)
        stacked = scaled_update.reshape(STACKED_RANK, count, block).transpose(1, 0, 2)
        based = frozen_up_weight[layer_index].reshape(count, block, HIDDEN_WIDTH)
        weighted_up_factor = adapter_up_stack[layer_index]

        def one_block(pair):
            a_block, b_block = pair
            delta = jnp.dot(a_block.T, weighted_up_factor, preferred_element_type=jnp.float32)
            return (b_block.astype(jnp.float32) + delta).astype(jnp.bfloat16)

        merged_layer = lax.map(one_block, (stacked, based)).reshape(MODEL_WIDTH, HIDDEN_WIDTH)
        results.append(merged_layer)
    return jnp.stack(results)
```

```python
import jax
import jax.numpy as jnp
from jax import lax
from jax.experimental import pallas as pl
from jax.experimental.pallas import tpu as pltpu
from jax.sharding import PartitionSpec as P

RANK = 16
TILE_AXES = ("row", "col")
ALL_AXES = ("client", "row", "col")
RING = 4
VMEM_LIMIT = 48 * 1024 * 1024


def place_of(x, y, z, core):
    return x * 32 + ((z % 2) * 2 + core) * 8 + y * 2 + z // 2


def shift(piece, dx=0, dy=0, dz=0, dcore=0, swap_on_core_1=False):
    pairs = []
    for x in range(RING):
        for y in range(RING):
            for z in range(RING):
                for core in range(2):
                    sy, sz = (dz, dy) if swap_on_core_1 and core else (dy, dz)
                    to = place_of(
                        (x + dx) % RING, (y + sy) % RING, (z + sz) % RING, (core + dcore) % 2
                    )
                    pairs.append((place_of(x, y, z, core), to))
    return lax.ppermute(piece, ALL_AXES, pairs)


def around(piece, axis):
    return jnp.concatenate(
        [piece]
        + [shift(piece, **{axis: RING - k}, swap_on_core_1=True) for k in range(1, RING)]
    )


def gather_down(scaled_here):
    layers, ranks, rows = scaled_here.shape
    piece = scaled_here.transpose(1, 0, 2).reshape(ranks, layers * rows)
    plane = around(around(piece, "dz"), "dy")
    return plane, shift(plane, dcore=1)


def gather_up(adapter_up_stack):
    layers, ranks, cols = adapter_up_stack.shape
    piece = adapter_up_stack.transpose(1, 0, 2).reshape(ranks, layers * cols)
    after, before = shift(piece, dx=RING - 1), shift(piece, dx=1)
    half = ranks // 2
    opposite = [shift(before[:half], dx=1), shift(after[half:], dx=RING - 1)]
    return jnp.concatenate([piece, after] + opposite + [before]).reshape(32, 8, layers * cols)


def sort_kernel(b_ref, out_ref):
    row, col = lax.axis_index("row"), lax.axis_index("col")
    x, y, z, core = lax.axis_index("client"), col // 2, (col % 2) * 2 + row // 2, row % 2
    for dcore in range(2):
        holder = lax.rem(core + dcore, 2)
        for second in range(RING):
            for first in range(RING):
                dy = jnp.where(holder == 0, second, first)
                dz = jnp.where(holder == 0, first, second)
                y_from, z_from = lax.rem(y + dy, RING), lax.rem(z + dz, RING)
                group = lax.rem(z_from, 2) * 2 + holder
                block = y_from * 2 + z_from // 2
                source = lax.rem(group - x + RING, RING) * 8 + block
                slot = (dcore * RING + second) * RING + first
                out_ref[slot] = b_ref[source]


def sort_up(b_blocks):
    return pl.pallas_call(
        sort_kernel,
        out_shape=jax.ShapeDtypeStruct(b_blocks.shape, b_blocks.dtype),
        compiler_params=pltpu.CompilerParams(vmem_limit_bytes=VMEM_LIMIT),
        cost_estimate=pl.CostEstimate(flops=0, bytes_accessed=4 * b_blocks.size, transcendentals=0),
    )(b_blocks)


def merge_kernel(base_ref, a00, a01, a10, a11, b_ref, out_ref):
    cols = base_ref.shape[-1]
    for layer, (own, other) in enumerate(((a00, a01), (a10, a11))):
        left = jnp.concatenate([own[...], other[...]], axis=0)
        right = b_ref[:, layer * cols : (layer + 1) * cols]
        delta = lax.dot_general(
            left, right, (((0,), (0,)), ((), ())), preferred_element_type=jnp.float32
        )
        merged = (base_ref[layer].astype(jnp.float32) + delta).astype(jnp.bfloat16)
        out_ref[:, layer] = merged.reshape(out_ref.shape[0], *out_ref.shape[2:])


def merge(base, own, other, b_sorted, parts):
    layers, rows, cols = base.shape
    part_rows = rows // parts
    tall = 256
    steps = rows // tall
    per = tall // part_rows
    half = own.shape[0]
    a_spec = [pl.BlockSpec((half, tall), lambda i, layer=layer: (0, layer * steps + i)) for layer in range(layers)]
    return pl.pallas_call(
        merge_kernel,
        grid=(steps,),
        in_specs=[
            pl.BlockSpec((layers, tall, cols), lambda i: (0, i, 0)),
            a_spec[0],
            a_spec[0],
            a_spec[1],
            a_spec[1],
            pl.BlockSpec(b_sorted.shape, lambda i: (0, 0)),
        ],
        out_specs=pl.BlockSpec((per, layers, part_rows, cols), lambda i: (i, 0, 0, 0)),
        out_shape=jax.ShapeDtypeStruct((parts, layers, part_rows, cols), jnp.bfloat16),
        compiler_params=pltpu.CompilerParams(vmem_limit_bytes=VMEM_LIMIT),
        cost_estimate=pl.CostEstimate(
            flops=2 * layers * rows * cols * 256, bytes_accessed=4 * base.size, transcendentals=0
        ),
    )(base, own, other, own, other, b_sorted)


def settle_kernel(in_ref, out_ref):
    parts, _, _, cols = in_ref.shape
    for part in range(parts):
        out_ref[0, :, part * cols : (part + 1) * cols] = in_ref[part, 0]


def settle(received):
    parts, layers, part_rows, cols = received.shape
    tall = 16
    return pl.pallas_call(
        settle_kernel,
        grid=(layers, part_rows // tall),
        in_specs=[pl.BlockSpec((parts, 1, tall, cols), lambda l, i: (0, l, i, 0))],
        out_specs=pl.BlockSpec((1, tall, parts * cols), lambda l, i: (l, i, 0)),
        out_shape=jax.ShapeDtypeStruct((layers, part_rows, parts * cols), jnp.bfloat16),
        compiler_params=pltpu.CompilerParams(vmem_limit_bytes=VMEM_LIMIT),
        cost_estimate=pl.CostEstimate(flops=0, bytes_accessed=4 * received.size, transcendentals=0),
    )(received)


def local(frozen_up_weight, adapter_down_stack, adapter_up_stack, participant_weight):
    parts = lax.axis_size(TILE_AXES)
    ranks_here = adapter_down_stack.shape[1]
    owner = (lax.axis_index(TILE_AXES) * ranks_here) // RANK
    weight = lax.dynamic_index_in_dim(participant_weight, owner, keepdims=False)
    scaled_here = (weight * adapter_down_stack.astype(jnp.float32)).astype(jnp.bfloat16)

    own, other = gather_down(scaled_here)
    b_sorted = sort_up(gather_up(adapter_up_stack)).reshape(own.shape[0] * 2, -1)
    merged = merge(frozen_up_weight, own, other, b_sorted, parts)
    received = lax.all_to_all(merged, TILE_AXES, split_axis=0, concat_axis=0, tiled=True)
    return settle(received)


def solution(mesh):
    return jax.shard_map(
        local,
        mesh=mesh,
        in_specs=(
            P(None, "client", ("row", "col")),
            P(None, ("row", "col"), "client"),
            P(None, "client", ("row", "col")),
            P(),
        ),
        out_specs=P(None, ("client", "row", "col"), None),
        check_vma=False,
    )
```

```python
import jax
import jax.numpy as jnp
from jax import lax
from jax.experimental import pallas as pl
from jax.experimental.pallas import tpu as pltpu
from jax.sharding import PartitionSpec as P

RANK = 16
TILE_AXES = ("row", "col")
ALL_AXES = ("client", "row", "col")
RING = 4
BLOCKS = 32
VMEM_LIMIT = 16 * 1024 * 1024


def place_of(x, y, z, core):
    return x * 32 + ((z % 2) * 2 + core) * 8 + y * 2 + z // 2


def spot_of(y, z, core):
    return (y % 2) * 16 + (y // 2) * 8 + (z // 2) * 4 + (z % 2) * 2 + core


def exchange(pieces):
    group = [0] * BLOCKS
    for y in range(RING):
        for z in range(RING):
            for core in range(2):
                group[spot_of(y, z, core)] = place_of(0, y, z, core)
    return lax.all_to_all(
        pieces, TILE_AXES, split_axis=0, concat_axis=0, axis_index_groups=[group], tiled=True
    )


def shift(piece, dx=0, dy=0, dz=0, dcore=0, swap_on_core_1=False):
    pairs = []
    for x in range(RING):
        for y in range(RING):
            for z in range(RING):
                for core in range(2):
                    sy, sz = (dz, dy) if swap_on_core_1 and core else (dy, dz)
                    to = place_of(
                        (x + dx) % RING, (y + sy) % RING, (z + sz) % RING, (core + dcore) % 2
                    )
                    pairs.append((place_of(x, y, z, core), to))
    return lax.ppermute(piece, ALL_AXES, pairs)


def around(piece, axis):
    return [piece] + [
        shift(piece, **{axis: RING - k}, swap_on_core_1=True) for k in range(1, RING)
    ]


def gather(base, adapter_down_stack, adapter_up_stack):
    layers, ranks, cols = adapter_up_stack.shape
    up = adapter_up_stack.reshape(1, layers, ranks // 8, 8, cols)
    near_up = jnp.concatenate([shift(up, dx=RING - 1), shift(up, dx=1)])
    touched = touch(base)
    mine, *others = around(adapter_down_stack[None], "dz")
    near_up, *others = gate([near_up] + others, [touched])
    ring = jnp.concatenate([mine] + others)
    own = around(ring, "dy")
    far_up = shift(up, dx=2)
    other = [shift(piece, dcore=1) for piece in own]
    b_groups = jnp.concatenate([up, near_up, far_up])
    return own + other, b_groups


def touch_kernel(base_ref, out_ref):
    out_ref[...] = jnp.zeros(out_ref.shape, out_ref.dtype)


def touch(base):
    vmem = pl.BlockSpec(memory_space=pltpu.VMEM)
    return pl.pallas_call(
        touch_kernel,
        in_specs=[vmem],
        out_specs=vmem,
        out_shape=jax.ShapeDtypeStruct((8, 128), jnp.float32),
        compiler_params=pltpu.CompilerParams(vmem_limit_bytes=VMEM_LIMIT),
        cost_estimate=pl.CostEstimate(flops=0, bytes_accessed=4 * base.size, transcendentals=0),
    )(base)


def gate(values, after):
    anywhere = pl.BlockSpec(memory_space=pl.ANY)
    specs = [anywhere] * len(values)
    return pl.pallas_call(
        lambda *refs: None,
        in_specs=specs + [anywhere] * len(after),
        out_specs=specs,
        out_shape=[jax.ShapeDtypeStruct(v.shape, v.dtype) for v in values],
        input_output_aliases={i: i for i in range(len(values))},
        compiler_params=pltpu.CompilerParams(vmem_limit_bytes=VMEM_LIMIT),
        cost_estimate=pl.CostEstimate(flops=0, bytes_accessed=0, transcendentals=0),
    )(*values, *after)


def sort_kernel(weight_ref, b_ref, out_ref, scale_ref):
    row, col = lax.axis_index("row"), lax.axis_index("col")
    x, y, z, core = lax.axis_index("client"), col // 2, (col % 2) * 2 + row // 2, row % 2
    for dcore in range(2):
        holder = lax.rem(core + dcore, 2)
        for second in range(RING):
            for first in range(RING):
                dy = jnp.where(holder == 0, second, first)
                dz = jnp.where(holder == 0, first, second)
                y_from, z_from = lax.rem(y + dy, RING), lax.rem(z + dz, RING)
                group = lax.rem(z_from, 2) * 2 + holder
                block = y_from * 2 + z_from // 2
                slot = (dcore * RING + second) * RING + first
                ahead = lax.rem(group - x + RING, RING)
                out_ref[:, slot] = b_ref[jnp.where(ahead < 2, ahead, 5 - ahead), :, block]
                scale_ref[slot] = jnp.full(
                    scale_ref.shape[1:], weight_ref[group * 4 + block // 2], jnp.float32
                )


def sort_up(participant_weight, b_groups):
    _, layers, _, _, cols = b_groups.shape
    vmem = pl.BlockSpec(memory_space=pltpu.VMEM)
    return pl.pallas_call(
        sort_kernel,
        in_specs=[pl.BlockSpec(memory_space=pltpu.SMEM), vmem],
        out_specs=[vmem, vmem],
        out_shape=[
            jax.ShapeDtypeStruct((layers, BLOCKS, 8, cols), b_groups.dtype),
            jax.ShapeDtypeStruct((BLOCKS, 8, 128), jnp.float32),
        ],
        compiler_params=pltpu.CompilerParams(vmem_limit_bytes=VMEM_LIMIT),
        cost_estimate=pl.CostEstimate(flops=0, bytes_accessed=4 * b_groups.size, transcendentals=0),
    )(participant_weight, b_groups)


def merge_kernel(base_ref, *refs):
    a_refs, (b_ref, scale_ref, out_ref) = refs[:-3], refs[-3:]
    layers, rows, cols = base_ref.shape
    part_rows = out_ref.shape[2]
    tall = 256
    per = tall // part_rows
    ranks = BLOCKS * 8
    scale = scale_ref[...].reshape(ranks, 128)
    scale = jnp.concatenate([scale] * (tall // 128), axis=1)
    for layer in range(layers):
        right = b_ref[layer].reshape(ranks, cols)

        @pl.loop(0, rows // tall, unroll=4)
        def _(i):
            span = pl.ds(pl.multiple_of(i * tall, tall), tall)
            left = jnp.concatenate(
                [ref[:, layer, :, span].reshape(-1, tall) for ref in a_refs]
            )
            left = (scale * left.astype(jnp.float32)).astype(jnp.bfloat16)
            delta = lax.dot_general(
                left, right, (((0,), (0,)), ((), ())), preferred_element_type=jnp.float32
            )
            merged = (base_ref[layer, span].astype(jnp.float32) + delta).astype(jnp.bfloat16)
            for part in range(per):
                place = i * per + part
                row, col = place // 8, lax.rem(place, 8)
                spot = spot_of(col // 2, lax.rem(col, 2) * 2 + row // 2, lax.rem(row, 2))
                out_ref[spot, layer] = merged[part * part_rows : (part + 1) * part_rows]


def merge(base, a_pieces, b_sorted, scale, parts):
    layers, rows, cols = base.shape
    vmem = pl.BlockSpec(memory_space=pltpu.VMEM)
    return pl.pallas_call(
        merge_kernel,
        in_specs=[vmem] * (len(a_pieces) + 3),
        out_specs=vmem,
        out_shape=jax.ShapeDtypeStruct((parts, layers, rows // parts, cols), jnp.bfloat16),
        compiler_params=pltpu.CompilerParams(vmem_limit_bytes=VMEM_LIMIT),
        cost_estimate=pl.CostEstimate(
            flops=2 * layers * rows * cols * 256, bytes_accessed=4 * base.size, transcendentals=0
        ),
    )(base, *a_pieces, b_sorted, scale)


def settle_kernel(in_ref, out_ref, sems):
    parts, layers, _, cols = in_ref.shape
    copies = [
        pltpu.make_async_copy(
            in_ref.at[spot_of(y, z, core), layer],
            out_ref.at[layer, :, pl.ds(place_of(0, y, z, core) * cols, cols)],
            sems.at[spot_of(y, z, core), layer],
        )
        for y in range(RING)
        for z in range(RING)
        for core in range(2)
        for layer in range(layers)
    ]
    for copy in copies:
        copy.start()
    for copy in copies:
        copy.wait()


def settle(received):
    parts, layers, part_rows, cols = received.shape
    return pl.pallas_call(
        settle_kernel,
        in_specs=[pl.BlockSpec(memory_space=pltpu.VMEM)],
        out_specs=pl.BlockSpec(memory_space=pl.ANY),
        out_shape=jax.ShapeDtypeStruct((layers, part_rows, parts * cols), jnp.bfloat16),
        scratch_shapes=[pltpu.SemaphoreType.DMA((parts, layers))],
        compiler_params=pltpu.CompilerParams(vmem_limit_bytes=VMEM_LIMIT),
        cost_estimate=pl.CostEstimate(flops=0, bytes_accessed=4 * received.size, transcendentals=0),
    )(received)


def local(frozen_up_weight, adapter_down_stack, adapter_up_stack, participant_weight):
    parts = lax.axis_size(TILE_AXES)
    a_pieces, b_groups = gather(frozen_up_weight, adapter_down_stack, adapter_up_stack)
    b_sorted, scale = sort_up(participant_weight, b_groups)
    merged = merge(frozen_up_weight, a_pieces, b_sorted, scale, parts)
    return settle(exchange(merged))


def solution(mesh):
    return jax.shard_map(
        local,
        mesh=mesh,
        in_specs=(
            P(None, "client", ("row", "col")),
            P(None, ("row", "col"), "client"),
            P(None, "client", ("row", "col")),
            P(),
        ),
        out_specs=P(None, ("client", "row", "col"), None),
        check_vma=False,
    )
```

```python
import jax
import jax.numpy as jnp
from jax import lax
from jax.experimental import pallas as pl
from jax.experimental.pallas import tpu as pltpu
from jax.sharding import PartitionSpec as P

RANK = 16
TILE_AXES = ("row", "col")
ALL_AXES = ("client", "row", "col")
RING = 4
BLOCKS = 32
VMEM_LIMIT = 16 * 1024 * 1024


def place_of(x, y, z, core):
    return x * 32 + ((z % 2) * 2 + core) * 8 + y * 2 + z // 2


def spot_of(y, z, core):
    return (y % 2) * 16 + (y // 2) * 8 + (z // 2) * 4 + (z % 2) * 2 + core


def exchange(pieces):
    group = [0] * BLOCKS
    for y in range(RING):
        for z in range(RING):
            for core in range(2):
                group[spot_of(y, z, core)] = place_of(0, y, z, core)
    return lax.all_to_all(
        pieces, TILE_AXES, split_axis=0, concat_axis=0, axis_index_groups=[group], tiled=True
    )


def shift(piece, dx=0, dy=0, dz=0, dcore=0, swap_on_core_1=False):
    pairs = []
    for x in range(RING):
        for y in range(RING):
            for z in range(RING):
                for core in range(2):
                    sy, sz = (dz, dy) if swap_on_core_1 and core else (dy, dz)
                    to = place_of(
                        (x + dx) % RING, (y + sy) % RING, (z + sz) % RING, (core + dcore) % 2
                    )
                    pairs.append((place_of(x, y, z, core), to))
    return lax.ppermute(piece, ALL_AXES, pairs)


def around(piece, axis):
    return [piece] + [
        shift(piece, **{axis: RING - k}, swap_on_core_1=True) for k in range(1, RING)
    ]


def facing(x, second):
    odd = x % 2
    return (x + 3 + 2 * odd) % RING if second else x + 1 - 2 * odd


def trade(piece, later):
    pairs = [
        (place_of(x, y, z, core), place_of(facing(x, core != later), y, z, core))
        for x in range(RING)
        for y in range(RING)
        for z in range(RING)
        for core in range(2)
    ]
    return lax.ppermute(piece, ALL_AXES, pairs)


def gather(base, adapter_down_stack, adapter_up_stack, participant_weight):
    layers, ranks, cols = adapter_up_stack.shape
    up = adapter_up_stack.reshape(1, layers, ranks // 8, 8, cols)
    near_up = jnp.concatenate([up, trade(up, False)])
    far_up = trade(near_up, True)
    mine, *others = around(adapter_down_stack[None], "dz")
    others = gate(others, [near_up, touch(base, [])])
    ring = jnp.concatenate([mine, *others])
    mine, *others = around(ring, "dy")
    own = [mine, *others]
    other = [shift(piece, dcore=1) for piece in own]
    near_sorted, scale = sort_near(participant_weight, near_up)
    return own + other, sort_far(far_up, near_sorted), scale


def touch_kernel(base_ref, *refs):
    out_ref = refs[-1]
    out_ref[...] = jnp.zeros(out_ref.shape, out_ref.dtype)


def touch(base, after):
    anywhere, vmem = pl.BlockSpec(memory_space=pl.ANY), pl.BlockSpec(memory_space=pltpu.VMEM)
    return pl.pallas_call(
        touch_kernel,
        in_specs=[vmem] + [anywhere] * len(after),
        out_specs=vmem,
        out_shape=jax.ShapeDtypeStruct((8, 128), jnp.float32),
        compiler_params=pltpu.CompilerParams(vmem_limit_bytes=VMEM_LIMIT),
        cost_estimate=pl.CostEstimate(flops=0, bytes_accessed=4 * base.size, transcendentals=0),
    )(base, *after)


def gate(values, after):
    anywhere = pl.BlockSpec(memory_space=pl.ANY)
    specs = [anywhere] * len(values)
    return pl.pallas_call(
        lambda *refs: None,
        in_specs=specs + [anywhere] * len(after),
        out_specs=specs,
        out_shape=[jax.ShapeDtypeStruct(v.shape, v.dtype) for v in values],
        input_output_aliases={i: i for i in range(len(values))},
        compiler_params=pltpu.CompilerParams(vmem_limit_bytes=VMEM_LIMIT),
        cost_estimate=pl.CostEstimate(flops=0, bytes_accessed=0, transcendentals=0),
    )(*values, *after)


def place_blocks(b_ref, out_ref, far):
    row, col = lax.axis_index("row"), lax.axis_index("col")
    x, y, z, core = lax.axis_index("client"), col // 2, (col % 2) * 2 + row // 2, row % 2
    early, late = facing(x, False), facing(x, True)
    first_pair = jnp.where(core == 0, early, late)
    last_pair = jnp.where(core == 0, late, early)
    groups = (last_pair, lax.rem(x + 2, RING)) if far else (x, first_pair)
    for i, group in enumerate(groups):
        holder = lax.rem(group, 2)
        for block in range(8):
            dy = lax.rem(block // 2 - y + RING, RING)
            dz = lax.rem(block % 2 * 2 + group // 2 - z + RING, RING)
            first, second = jnp.where(holder == 0, dz, dy), jnp.where(holder == 0, dy, dz)
            slot = (lax.rem(holder + core, 2) * RING + second) * RING + first
            out_ref[:, slot] = b_ref[i, :, block]


def near_kernel(weight_ref, near_ref, out_ref, scale_ref):
    place_blocks(near_ref, out_ref, False)
    row, col = lax.axis_index("row"), lax.axis_index("col")
    y, z, core = col // 2, (col % 2) * 2 + row // 2, row % 2
    for dcore in range(2):
        holder = lax.rem(core + dcore, 2)
        for second in range(RING):
            for first in range(RING):
                dy = jnp.where(holder == 0, second, first)
                dz = jnp.where(holder == 0, first, second)
                y_from, z_from = lax.rem(y + dy, RING), lax.rem(z + dz, RING)
                client = (lax.rem(z_from, 2) * 2 + holder) * 4 + y_from
                scale_ref[(dcore * RING + second) * RING + first] = jnp.full(
                    scale_ref.shape[1:], weight_ref[client], jnp.float32
                )


def sort_near(participant_weight, near_up):
    _, layers, _, _, cols = near_up.shape
    vmem = pl.BlockSpec(memory_space=pltpu.VMEM)
    return pl.pallas_call(
        near_kernel,
        in_specs=[pl.BlockSpec(memory_space=pltpu.SMEM), vmem],
        out_specs=[vmem, vmem],
        out_shape=[
            jax.ShapeDtypeStruct((layers, BLOCKS, 8, cols), near_up.dtype),
            jax.ShapeDtypeStruct((BLOCKS, 8, 128), jnp.float32),
        ],
        compiler_params=pltpu.CompilerParams(vmem_limit_bytes=VMEM_LIMIT),
        cost_estimate=pl.CostEstimate(flops=0, bytes_accessed=4 * near_up.size, transcendentals=0),
    )(participant_weight, near_up)


def far_kernel(far_ref, _, out_ref):
    place_blocks(far_ref, out_ref, True)


def sort_far(far_up, near_sorted):
    vmem = pl.BlockSpec(memory_space=pltpu.VMEM)
    return pl.pallas_call(
        far_kernel,
        in_specs=[vmem, vmem],
        out_specs=vmem,
        out_shape=jax.ShapeDtypeStruct(near_sorted.shape, near_sorted.dtype),
        input_output_aliases={1: 0},
        compiler_params=pltpu.CompilerParams(vmem_limit_bytes=VMEM_LIMIT),
        cost_estimate=pl.CostEstimate(flops=0, bytes_accessed=4 * far_up.size, transcendentals=0),
    )(far_up, near_sorted)


def merge_kernel(base_ref, *refs):
    a_refs, (b_ref, scale_ref, out_ref) = refs[:-3], refs[-3:]
    layers, rows, cols = base_ref.shape
    part_rows = out_ref.shape[2]
    tall = 256
    per = tall // part_rows
    ranks = BLOCKS * 8
    scale = scale_ref[...].reshape(ranks, 128)
    scale = jnp.concatenate([scale] * (tall // 128), axis=1)
    for layer in range(layers):
        right = b_ref[layer].reshape(ranks, cols)

        @pl.loop(0, rows // tall, unroll=8)
        def _(i):
            span = pl.ds(pl.multiple_of(i * tall, tall), tall)
            left = jnp.concatenate(
                [ref[:, layer, :, span].reshape(-1, tall) for ref in a_refs]
            )
            left = (scale * left.astype(jnp.float32)).astype(jnp.bfloat16)
            delta = lax.dot_general(
                left, right, (((0,), (0,)), ((), ())), preferred_element_type=jnp.float32
            )
            merged = (base_ref[layer, span].astype(jnp.float32) + delta).astype(jnp.bfloat16)
            for part in range(per):
                place = i * per + part
                row, col = place // 8, lax.rem(place, 8)
                spot = spot_of(col // 2, lax.rem(col, 2) * 2 + row // 2, lax.rem(row, 2))
                out_ref[spot, layer] = merged[part * part_rows : (part + 1) * part_rows]


def merge(base, a_pieces, b_sorted, scale, parts):
    layers, rows, cols = base.shape
    vmem = pl.BlockSpec(memory_space=pltpu.VMEM)
    return pl.pallas_call(
        merge_kernel,
        in_specs=[vmem] * (len(a_pieces) + 3),
        out_specs=vmem,
        out_shape=jax.ShapeDtypeStruct((parts, layers, rows // parts, cols), jnp.bfloat16),
        compiler_params=pltpu.CompilerParams(vmem_limit_bytes=VMEM_LIMIT),
        cost_estimate=pl.CostEstimate(
            flops=2 * layers * rows * cols * 256, bytes_accessed=4 * base.size, transcendentals=0
        ),
    )(base, *a_pieces, b_sorted, scale)


def settle_kernel(in_ref, out_ref, lines, sems):
    _, layers, part_rows, cols = in_ref.shape
    tall = lines.shape[1]
    copies = []
    for layer in range(layers):
        for first in range(0, part_rows, tall):
            slot = len(copies)
            for y in range(RING):
                for z in range(RING):
                    for core in range(2):
                        left = place_of(0, y, z, core) * cols
                        lines[slot, :, left : left + cols] = in_ref[
                            spot_of(y, z, core), layer, first : first + tall
                        ]
            copies.append(
                pltpu.make_async_copy(
                    lines.at[slot], out_ref.at[layer, pl.ds(first, tall)], sems.at[slot]
                )
            )
            copies[-1].start()
    for copy in copies:
        copy.wait()


def settle(received):
    parts, layers, part_rows, cols = received.shape
    tall = 16
    slots = layers * part_rows // tall
    return pl.pallas_call(
        settle_kernel,
        in_specs=[pl.BlockSpec(memory_space=pltpu.VMEM)],
        out_specs=pl.BlockSpec(memory_space=pl.ANY),
        out_shape=jax.ShapeDtypeStruct((layers, part_rows, parts * cols), jnp.bfloat16),
        scratch_shapes=[
            pltpu.VMEM((slots, tall, parts * cols), jnp.bfloat16),
            pltpu.SemaphoreType.DMA((slots,)),
        ],
        compiler_params=pltpu.CompilerParams(vmem_limit_bytes=VMEM_LIMIT),
        cost_estimate=pl.CostEstimate(flops=0, bytes_accessed=4 * received.size, transcendentals=0),
    )(received)


def local(frozen_up_weight, adapter_down_stack, adapter_up_stack, participant_weight):
    parts = lax.axis_size(TILE_AXES)
    a_pieces, b_sorted, scale = gather(
        frozen_up_weight, adapter_down_stack, adapter_up_stack, participant_weight
    )
    merged = merge(frozen_up_weight, a_pieces, b_sorted, scale, parts)
    return settle(exchange(merged))


def solution(mesh):
    return jax.shard_map(
        local,
        mesh=mesh,
        in_specs=(
            P(None, "client", ("row", "col")),
            P(None, ("row", "col"), "client"),
            P(None, "client", ("row", "col")),
            P(),
        ),
        out_specs=P(None, ("client", "row", "col"), None),
        check_vma=False,
    )
```

```python
import jax
import jax.numpy as jnp
from jax import lax
from jax.experimental import pallas as pl
from jax.experimental.pallas import tpu as pltpu
from jax.sharding import PartitionSpec as P

RANK = 16
TILE_AXES = ("row", "col")
ALL_AXES = ("client", "row", "col")
RING = 4
BLOCKS = 32
VMEM_LIMIT = 16 * 1024 * 1024


def place_of(x, y, z, core):
    return x * 32 + ((z % 2) * 2 + core) * 8 + y * 2 + z // 2


def spot_of(y, z, core):
    return z * 8 + (y % 2) * 4 + core * 2 + y // 2


def exchange(pieces):
    group = [0] * BLOCKS
    for y in range(RING):
        for z in range(RING):
            for core in range(2):
                group[spot_of(y, z, core)] = place_of(0, y, z, core)
    return lax.all_to_all(
        pieces, TILE_AXES, split_axis=0, concat_axis=0, axis_index_groups=[group], tiled=True
    )


def shift(piece, dx=0, dy=0, dz=0, dcore=0, swap_on_core_1=False):
    pairs = []
    for x in range(RING):
        for y in range(RING):
            for z in range(RING):
                for core in range(2):
                    sy, sz = (dz, dy) if swap_on_core_1 and core else (dy, dz)
                    to = place_of(
                        (x + dx) % RING, (y + sy) % RING, (z + sz) % RING, (core + dcore) % 2
                    )
                    pairs.append((place_of(x, y, z, core), to))
    return lax.ppermute(piece, ALL_AXES, pairs)


def around(piece, axis):
    return [piece] + [
        shift(piece, **{axis: RING - k}, swap_on_core_1=True) for k in range(1, RING)
    ]


def facing(x, second):
    odd = x % 2
    return (x + 3 + 2 * odd) % RING if second else x + 1 - 2 * odd


def trade(piece, later):
    pairs = [
        (place_of(x, y, z, core), place_of(facing(x, core != later), y, z, core))
        for x in range(RING)
        for y in range(RING)
        for z in range(RING)
        for core in range(2)
    ]
    return lax.ppermute(piece, ALL_AXES, pairs)


def gather(base, adapter_down_stack, adapter_up_stack, participant_weight):
    layers, ranks, cols = adapter_up_stack.shape
    up = adapter_up_stack.reshape(1, layers, ranks // 8, 8, cols)
    near_up = jnp.concatenate([up, trade(up, False)])
    far_up = trade(near_up, True)
    (here,) = stage([adapter_down_stack[None]])
    _, *others = around(adapter_down_stack[None], "dz")
    ring = jnp.concatenate([here, *others])
    mine, *others = around(ring, "dy")
    near_sorted, scale = sort_near(participant_weight, near_up)
    b_sorted = sort_far(far_up, near_sorted)
    touched = touch(base, [])
    others = [gate([piece], [touched, far_up])[0] for piece in others]
    own = [mine, *others]
    other = [shift(piece, dcore=1) for piece in own]
    return own + other, b_sorted, scale


def stage_kernel(*refs):
    half = len(refs) // 2
    for in_ref, out_ref in zip(refs[:half], refs[half:]):
        out_ref[...] = in_ref[...]


def stage(arrays):
    vmem = pl.BlockSpec(memory_space=pltpu.VMEM)
    return pl.pallas_call(
        stage_kernel,
        in_specs=[vmem] * len(arrays),
        out_specs=[vmem] * len(arrays),
        out_shape=[jax.ShapeDtypeStruct(a.shape, a.dtype) for a in arrays],
        compiler_params=pltpu.CompilerParams(vmem_limit_bytes=VMEM_LIMIT),
        cost_estimate=pl.CostEstimate(flops=0, bytes_accessed=1 << 20, transcendentals=0),
    )(*arrays)


def touch_kernel(base_ref, *refs):
    out_ref = refs[-1]
    out_ref[...] = jnp.zeros(out_ref.shape, out_ref.dtype)


def touch(base, after):
    anywhere, vmem = pl.BlockSpec(memory_space=pl.ANY), pl.BlockSpec(memory_space=pltpu.VMEM)
    return pl.pallas_call(
        touch_kernel,
        in_specs=[vmem] + [anywhere] * len(after),
        out_specs=vmem,
        out_shape=jax.ShapeDtypeStruct((8, 128), jnp.float32),
        compiler_params=pltpu.CompilerParams(vmem_limit_bytes=VMEM_LIMIT),
        cost_estimate=pl.CostEstimate(flops=0, bytes_accessed=4 * base.size, transcendentals=0),
    )(base, *after)


def gate(values, after):
    anywhere = pl.BlockSpec(memory_space=pl.ANY)
    specs = [anywhere] * len(values)
    return pl.pallas_call(
        lambda *refs: None,
        in_specs=specs + [anywhere] * len(after),
        out_specs=specs,
        out_shape=[jax.ShapeDtypeStruct(v.shape, v.dtype) for v in values],
        input_output_aliases={i: i for i in range(len(values))},
        compiler_params=pltpu.CompilerParams(vmem_limit_bytes=VMEM_LIMIT),
        cost_estimate=pl.CostEstimate(flops=0, bytes_accessed=0, transcendentals=0),
    )(*values, *after)


def place_blocks(b_ref, out_ref, far):
    row, col = lax.axis_index("row"), lax.axis_index("col")
    x, y, z, core = lax.axis_index("client"), col // 2, (col % 2) * 2 + row // 2, row % 2
    early, late = facing(x, False), facing(x, True)
    first_pair = jnp.where(core == 0, early, late)
    last_pair = jnp.where(core == 0, late, early)
    groups = (last_pair, lax.rem(x + 2, RING)) if far else (x, first_pair)
    for i, group in enumerate(groups):
        holder = lax.rem(group, 2)
        for block in range(8):
            dy = lax.rem(block // 2 - y + RING, RING)
            dz = lax.rem(block % 2 * 2 + group // 2 - z + RING, RING)
            first, second = jnp.where(holder == 0, dz, dy), jnp.where(holder == 0, dy, dz)
            slot = (lax.rem(holder + core, 2) * RING + second) * RING + first
            out_ref[:, slot] = b_ref[i, :, block]


def near_kernel(weight_ref, near_ref, out_ref, scale_ref):
    place_blocks(near_ref, out_ref, False)
    row, col = lax.axis_index("row"), lax.axis_index("col")
    y, z, core = col // 2, (col % 2) * 2 + row // 2, row % 2
    for dcore in range(2):
        holder = lax.rem(core + dcore, 2)
        for second in range(RING):
            for first in range(RING):
                dy = jnp.where(holder == 0, second, first)
                dz = jnp.where(holder == 0, first, second)
                y_from, z_from = lax.rem(y + dy, RING), lax.rem(z + dz, RING)
                client = (lax.rem(z_from, 2) * 2 + holder) * 4 + y_from
                scale_ref[(dcore * RING + second) * RING + first] = jnp.full(
                    scale_ref.shape[1:], weight_ref[client], jnp.float32
                )


def sort_near(participant_weight, near_up):
    _, layers, _, _, cols = near_up.shape
    vmem = pl.BlockSpec(memory_space=pltpu.VMEM)
    return pl.pallas_call(
        near_kernel,
        in_specs=[pl.BlockSpec(memory_space=pltpu.SMEM), vmem],
        out_specs=[vmem, vmem],
        out_shape=[
            jax.ShapeDtypeStruct((layers, BLOCKS, 8, cols), near_up.dtype),
            jax.ShapeDtypeStruct((BLOCKS, 8, 128), jnp.float32),
        ],
        compiler_params=pltpu.CompilerParams(vmem_limit_bytes=VMEM_LIMIT),
        cost_estimate=pl.CostEstimate(flops=0, bytes_accessed=4 * near_up.size, transcendentals=0),
    )(participant_weight, near_up)


def far_kernel(far_ref, _, out_ref):
    place_blocks(far_ref, out_ref, True)


def sort_far(far_up, near_sorted):
    vmem = pl.BlockSpec(memory_space=pltpu.VMEM)
    return pl.pallas_call(
        far_kernel,
        in_specs=[vmem, vmem],
        out_specs=vmem,
        out_shape=jax.ShapeDtypeStruct(near_sorted.shape, near_sorted.dtype),
        input_output_aliases={1: 0},
        compiler_params=pltpu.CompilerParams(vmem_limit_bytes=VMEM_LIMIT),
        cost_estimate=pl.CostEstimate(flops=0, bytes_accessed=4 * far_up.size, transcendentals=0),
    )(far_up, near_sorted)


def merge_kernel(base_ref, *refs):
    a_refs, (b_ref, scale_ref, out_ref) = refs[:-3], refs[-3:]
    layers, rows, cols = base_ref.shape
    part_rows = out_ref.shape[2]
    tall = 256
    per = tall // part_rows
    ranks = BLOCKS * 8
    scale = scale_ref[...].reshape(ranks, 128)
    scale = jnp.concatenate([scale] * (tall // 128), axis=1)
    for layer in range(layers):
        right = b_ref[layer].reshape(ranks, cols)

        @pl.loop(0, rows // tall, unroll=8)
        def _(i):
            span = pl.ds(pl.multiple_of(i * tall, tall), tall)
            left = jnp.concatenate(
                [ref[:, layer, :, span].reshape(-1, tall) for ref in a_refs]
            )
            left = (scale * left.astype(jnp.float32)).astype(jnp.bfloat16)
            delta = lax.dot_general(
                left, right, (((0,), (0,)), ((), ())), preferred_element_type=jnp.float32
            )
            merged = (base_ref[layer, span].astype(jnp.float32) + delta).astype(jnp.bfloat16)
            for part in range(per):
                place = i * per + part
                row, col = place // 8, lax.rem(place, 8)
                spot = spot_of(col // 2, lax.rem(col, 2) * 2 + row // 2, lax.rem(row, 2))
                out_ref[spot, layer] = merged[part * part_rows : (part + 1) * part_rows]


def merge(base, a_pieces, b_sorted, scale, parts):
    layers, rows, cols = base.shape
    vmem = pl.BlockSpec(memory_space=pltpu.VMEM)
    return pl.pallas_call(
        merge_kernel,
        in_specs=[vmem] * (len(a_pieces) + 3),
        out_specs=vmem,
        out_shape=jax.ShapeDtypeStruct((parts, layers, rows // parts, cols), jnp.bfloat16),
        compiler_params=pltpu.CompilerParams(vmem_limit_bytes=VMEM_LIMIT),
        cost_estimate=pl.CostEstimate(
            flops=2 * layers * rows * cols * 256, bytes_accessed=4 * base.size, transcendentals=0
        ),
    )(base, *a_pieces, b_sorted, scale)


def settle_kernel(in_ref, out_ref, lines, sems):
    _, layers, part_rows, cols = in_ref.shape
    tall = lines.shape[1]
    copies = []
    for layer in range(layers):
        for first in range(0, part_rows, tall):
            slot = len(copies)
            for y in range(RING):
                for z in range(RING):
                    for core in range(2):
                        left = place_of(0, y, z, core) * cols
                        lines[slot, :, left : left + cols] = in_ref[
                            spot_of(y, z, core), layer, first : first + tall
                        ]
            copies.append(
                pltpu.make_async_copy(
                    lines.at[slot], out_ref.at[layer, pl.ds(first, tall)], sems.at[slot]
                )
            )
            copies[-1].start()
    for copy in copies:
        copy.wait()


def settle(received):
    parts, layers, part_rows, cols = received.shape
    tall = 16
    slots = layers * part_rows // tall
    return pl.pallas_call(
        settle_kernel,
        in_specs=[pl.BlockSpec(memory_space=pltpu.VMEM)],
        out_specs=pl.BlockSpec(memory_space=pl.ANY),
        out_shape=jax.ShapeDtypeStruct((layers, part_rows, parts * cols), jnp.bfloat16),
        scratch_shapes=[
            pltpu.VMEM((slots, tall, parts * cols), jnp.bfloat16),
            pltpu.SemaphoreType.DMA((slots,)),
        ],
        compiler_params=pltpu.CompilerParams(vmem_limit_bytes=VMEM_LIMIT),
        cost_estimate=pl.CostEstimate(flops=0, bytes_accessed=4 * received.size, transcendentals=0),
    )(received)


def local(frozen_up_weight, adapter_down_stack, adapter_up_stack, participant_weight):
    parts = lax.axis_size(TILE_AXES)
    a_pieces, b_sorted, scale = gather(
        frozen_up_weight, adapter_down_stack, adapter_up_stack, participant_weight
    )
    merged = merge(frozen_up_weight, a_pieces, b_sorted, scale, parts)
    return settle(exchange(merged))


def solution(mesh):
    return jax.shard_map(
        local,
        mesh=mesh,
        in_specs=(
            P(None, "client", ("row", "col")),
            P(None, ("row", "col"), "client"),
            P(None, "client", ("row", "col")),
            P(),
        ),
        out_specs=P(None, ("client", "row", "col"), None),
        check_vma=False,
    )
```

```python
import jax
import jax.numpy as jnp
from jax import lax
from jax.experimental import pallas as pl
from jax.experimental.pallas import tpu as pltpu
from jax.sharding import PartitionSpec as P

RANK = 16
TILE_AXES = ("row", "col")
ALL_AXES = ("client", "row", "col")
RING = 4
BLOCKS = 32
VMEM_LIMIT = 16 * 1024 * 1024


def place_of(x, y, z, core):
    return x * 32 + ((z % 2) * 2 + core) * 8 + y * 2 + z // 2


def spot_of(y, z, core):
    return z * 8 + (y % 2) * 4 + core * 2 + y // 2


def exchange(pieces):
    group = [0] * BLOCKS
    for y in range(RING):
        for z in range(RING):
            for core in range(2):
                group[spot_of(y, z, core)] = place_of(0, y, z, core)
    return lax.all_to_all(
        pieces, TILE_AXES, split_axis=0, concat_axis=0, axis_index_groups=[group], tiled=True
    )


def shift(piece, dx=0, dy=0, dz=0, dcore=0, swap_on_core_1=False):
    pairs = []
    for x in range(RING):
        for y in range(RING):
            for z in range(RING):
                for core in range(2):
                    sy, sz = (dz, dy) if swap_on_core_1 and core else (dy, dz)
                    to = place_of(
                        (x + dx) % RING, (y + sy) % RING, (z + sz) % RING, (core + dcore) % 2
                    )
                    pairs.append((place_of(x, y, z, core), to))
    return lax.ppermute(piece, ALL_AXES, pairs)


def around(piece, axis):
    return [piece] + [
        shift(piece, **{axis: RING - k}, swap_on_core_1=True) for k in range(1, RING)
    ]


def facing(x, second):
    odd = x % 2
    return (x + 3 + 2 * odd) % RING if second else x + 1 - 2 * odd


def trade(piece, later):
    pairs = [
        (place_of(x, y, z, core), place_of(facing(x, core != later), y, z, core))
        for x in range(RING)
        for y in range(RING)
        for z in range(RING)
        for core in range(2)
    ]
    return lax.ppermute(piece, ALL_AXES, pairs)


def gather(base, adapter_down_stack, adapter_up_stack, participant_weight):
    layers, ranks, cols = adapter_up_stack.shape
    up = adapter_up_stack.reshape(1, layers, ranks // 8, 8, cols)
    near_up = jnp.concatenate([up, trade(up, False)])
    far_up = trade(near_up, True)
    (here,) = stage([adapter_down_stack[None]])
    _, *others = around(adapter_down_stack[None], "dz")
    ring = jnp.concatenate([here, *others])
    mine, *others = around(ring, "dy")
    near_sorted, scale = sort_near(participant_weight, near_up)
    b_sorted = sort_far(far_up, near_sorted)
    touched = touch(base, [])
    others = [gate([piece], [touched, b_sorted])[0] for piece in others]
    own = [mine, *others]
    other = [shift(piece, dcore=1) for piece in own]
    return own + other, b_sorted, scale


def stage_kernel(*refs):
    half = len(refs) // 2
    for in_ref, out_ref in zip(refs[:half], refs[half:]):
        out_ref[...] = in_ref[...]


def stage(arrays):
    vmem = pl.BlockSpec(memory_space=pltpu.VMEM)
    return pl.pallas_call(
        stage_kernel,
        in_specs=[vmem] * len(arrays),
        out_specs=[vmem] * len(arrays),
        out_shape=[jax.ShapeDtypeStruct(a.shape, a.dtype) for a in arrays],
        compiler_params=pltpu.CompilerParams(vmem_limit_bytes=VMEM_LIMIT),
        cost_estimate=pl.CostEstimate(flops=0, bytes_accessed=1 << 20, transcendentals=0),
    )(*arrays)


def touch_kernel(base_ref, *refs):
    out_ref = refs[-1]
    out_ref[...] = jnp.zeros(out_ref.shape, out_ref.dtype)


def touch(base, after):
    anywhere, vmem = pl.BlockSpec(memory_space=pl.ANY), pl.BlockSpec(memory_space=pltpu.VMEM)
    return pl.pallas_call(
        touch_kernel,
        in_specs=[vmem] + [anywhere] * len(after),
        out_specs=vmem,
        out_shape=jax.ShapeDtypeStruct((8, 128), jnp.float32),
        compiler_params=pltpu.CompilerParams(vmem_limit_bytes=VMEM_LIMIT),
        cost_estimate=pl.CostEstimate(flops=0, bytes_accessed=4 * base.size, transcendentals=0),
    )(base, *after)


def gate(values, after):
    anywhere = pl.BlockSpec(memory_space=pl.ANY)
    specs = [anywhere] * len(values)
    return pl.pallas_call(
        lambda *refs: None,
        in_specs=specs + [anywhere] * len(after),
        out_specs=specs,
        out_shape=[jax.ShapeDtypeStruct(v.shape, v.dtype) for v in values],
        input_output_aliases={i: i for i in range(len(values))},
        compiler_params=pltpu.CompilerParams(vmem_limit_bytes=VMEM_LIMIT),
        cost_estimate=pl.CostEstimate(flops=0, bytes_accessed=0, transcendentals=0),
    )(*values, *after)


def place_blocks(b_ref, out_ref, far):
    row, col = lax.axis_index("row"), lax.axis_index("col")
    x, y, z, core = lax.axis_index("client"), col // 2, (col % 2) * 2 + row // 2, row % 2
    early, late = facing(x, False), facing(x, True)
    first_pair = jnp.where(core == 0, early, late)
    last_pair = jnp.where(core == 0, late, early)
    groups = (last_pair, lax.rem(x + 2, RING)) if far else (x, first_pair)
    for i, group in enumerate(groups):
        holder = lax.rem(group, 2)
        for block in range(8):
            dy = lax.rem(block // 2 - y + RING, RING)
            dz = lax.rem(block % 2 * 2 + group // 2 - z + RING, RING)
            first, second = jnp.where(holder == 0, dz, dy), jnp.where(holder == 0, dy, dz)
            slot = (lax.rem(holder + core, 2) * RING + second) * RING + first
            out_ref[:, slot] = b_ref[i, :, block]


def near_kernel(weight_ref, near_ref, out_ref, scale_ref):
    place_blocks(near_ref, out_ref, False)
    row, col = lax.axis_index("row"), lax.axis_index("col")
    y, z, core = col // 2, (col % 2) * 2 + row // 2, row % 2
    for dcore in range(2):
        holder = lax.rem(core + dcore, 2)
        for second in range(RING):
            for first in range(RING):
                dy = jnp.where(holder == 0, second, first)
                dz = jnp.where(holder == 0, first, second)
                y_from, z_from = lax.rem(y + dy, RING), lax.rem(z + dz, RING)
                client = (lax.rem(z_from, 2) * 2 + holder) * 4 + y_from
                scale_ref[(dcore * RING + second) * RING + first] = jnp.full(
                    scale_ref.shape[1:], weight_ref[client], jnp.float32
                )


def sort_near(participant_weight, near_up):
    _, layers, _, _, cols = near_up.shape
    vmem = pl.BlockSpec(memory_space=pltpu.VMEM)
    return pl.pallas_call(
        near_kernel,
        in_specs=[pl.BlockSpec(memory_space=pltpu.SMEM), vmem],
        out_specs=[vmem, vmem],
        out_shape=[
            jax.ShapeDtypeStruct((layers, BLOCKS, 8, cols), near_up.dtype),
            jax.ShapeDtypeStruct((BLOCKS, 8, 128), jnp.float32),
        ],
        compiler_params=pltpu.CompilerParams(vmem_limit_bytes=VMEM_LIMIT),
        cost_estimate=pl.CostEstimate(flops=0, bytes_accessed=4 * near_up.size, transcendentals=0),
    )(participant_weight, near_up)


def far_kernel(far_ref, _, out_ref):
    place_blocks(far_ref, out_ref, True)


def sort_far(far_up, near_sorted):
    vmem = pl.BlockSpec(memory_space=pltpu.VMEM)
    return pl.pallas_call(
        far_kernel,
        in_specs=[vmem, vmem],
        out_specs=vmem,
        out_shape=jax.ShapeDtypeStruct(near_sorted.shape, near_sorted.dtype),
        input_output_aliases={1: 0},
        compiler_params=pltpu.CompilerParams(vmem_limit_bytes=VMEM_LIMIT),
        cost_estimate=pl.CostEstimate(flops=0, bytes_accessed=4 * far_up.size, transcendentals=0),
    )(far_up, near_sorted)


def merge_kernel(base_ref, *refs):
    a_refs, (b_ref, scale_ref, out_ref) = refs[:-3], refs[-3:]
    layers, rows, cols = base_ref.shape
    part_rows = out_ref.shape[2]
    tall = 256
    per = tall // part_rows
    ranks = BLOCKS * 8
    scale = scale_ref[...].reshape(ranks, 128)
    scale = jnp.concatenate([scale] * (tall // 128), axis=1)
    rights = [b_ref[layer].reshape(ranks, cols) for layer in range(layers)]

    @pl.loop(0, rows // tall, unroll=8)
    def _(i):
        span = pl.ds(pl.multiple_of(i * tall, tall), tall)
        for layer in range(layers):
            left = jnp.concatenate(
                [ref[:, layer, :, span].reshape(-1, tall) for ref in a_refs]
            )
            left = (scale * left.astype(jnp.float32)).astype(jnp.bfloat16)
            delta = lax.dot_general(
                left, rights[layer], (((0,), (0,)), ((), ())), preferred_element_type=jnp.float32
            )
            merged = (base_ref[layer, span].astype(jnp.float32) + delta).astype(jnp.bfloat16)
            for part in range(per):
                place = i * per + part
                row, col = place // 8, lax.rem(place, 8)
                spot = spot_of(col // 2, lax.rem(col, 2) * 2 + row // 2, lax.rem(row, 2))
                out_ref[spot, layer] = merged[part * part_rows : (part + 1) * part_rows]


def merge(base, a_pieces, b_sorted, scale, parts):
    layers, rows, cols = base.shape
    vmem = pl.BlockSpec(memory_space=pltpu.VMEM)
    return pl.pallas_call(
        merge_kernel,
        in_specs=[vmem] * (len(a_pieces) + 3),
        out_specs=vmem,
        out_shape=jax.ShapeDtypeStruct((parts, layers, rows // parts, cols), jnp.bfloat16),
        compiler_params=pltpu.CompilerParams(vmem_limit_bytes=VMEM_LIMIT),
        cost_estimate=pl.CostEstimate(
            flops=2 * layers * rows * cols * 256, bytes_accessed=4 * base.size, transcendentals=0
        ),
    )(base, *a_pieces, b_sorted, scale)


def settle_kernel(in_ref, out_ref, lines, sems):
    _, layers, part_rows, cols = in_ref.shape
    tall = lines.shape[1]
    copies = []
    for layer in range(layers):
        for first in range(0, part_rows, tall):
            slot = len(copies)
            for y in range(RING):
                for z in range(RING):
                    for core in range(2):
                        left = place_of(0, y, z, core) * cols
                        lines[slot, :, left : left + cols] = in_ref[
                            spot_of(y, z, core), layer, first : first + tall
                        ]
            copies.append(
                pltpu.make_async_copy(
                    lines.at[slot], out_ref.at[layer, pl.ds(first, tall)], sems.at[slot]
                )
            )
            copies[-1].start()
    for copy in copies:
        copy.wait()


def settle(received):
    parts, layers, part_rows, cols = received.shape
    tall = 16
    slots = layers * part_rows // tall
    return pl.pallas_call(
        settle_kernel,
        in_specs=[pl.BlockSpec(memory_space=pltpu.VMEM)],
        out_specs=pl.BlockSpec(memory_space=pl.ANY),
        out_shape=jax.ShapeDtypeStruct((layers, part_rows, parts * cols), jnp.bfloat16),
        scratch_shapes=[
            pltpu.VMEM((slots, tall, parts * cols), jnp.bfloat16),
            pltpu.SemaphoreType.DMA((slots,)),
        ],
        compiler_params=pltpu.CompilerParams(vmem_limit_bytes=VMEM_LIMIT),
        cost_estimate=pl.CostEstimate(flops=0, bytes_accessed=4 * received.size, transcendentals=0),
    )(received)


def local(frozen_up_weight, adapter_down_stack, adapter_up_stack, participant_weight):
    parts = lax.axis_size(TILE_AXES)
    a_pieces, b_sorted, scale = gather(
        frozen_up_weight, adapter_down_stack, adapter_up_stack, participant_weight
    )
    merged = merge(frozen_up_weight, a_pieces, b_sorted, scale, parts)
    return settle(exchange(merged))


def solution(mesh):
    return jax.shard_map(
        local,
        mesh=mesh,
        in_specs=(
            P(None, "client", ("row", "col")),
            P(None, ("row", "col"), "client"),
            P(None, "client", ("row", "col")),
            P(),
        ),
        out_specs=P(None, ("client", "row", "col"), None),
        check_vma=False,
    )
```

```python
import jax
import jax.numpy as jnp
from jax import lax
from jax.experimental import pallas as pl
from jax.experimental.pallas import tpu as pltpu
from jax.sharding import PartitionSpec as P

RANK = 16
TILE_AXES = ("row", "col")
ALL_AXES = ("client", "row", "col")
RING = 4
BLOCKS = 32
VMEM_LIMIT = 16 * 1024 * 1024


def place_of(x, y, z, core):
    return x * 32 + ((z % 2) * 2 + core) * 8 + y * 2 + z // 2


def spot_of(y, z, core):
    return (z // 2) * 16 + core * 8 + (z % 2) * 4 + (y % 2) * 2 + y // 2


def exchange(pieces):
    group = [0] * BLOCKS
    for y in range(RING):
        for z in range(RING):
            for core in range(2):
                group[spot_of(y, z, core)] = place_of(0, y, z, core)
    return lax.all_to_all(
        pieces, TILE_AXES, split_axis=0, concat_axis=0, axis_index_groups=[group], tiled=True
    )


def shift(piece, dx=0, dy=0, dz=0, dcore=0, swap_on_core_1=False):
    pairs = []
    for x in range(RING):
        for y in range(RING):
            for z in range(RING):
                for core in range(2):
                    sy, sz = (dz, dy) if swap_on_core_1 and core else (dy, dz)
                    to = place_of(
                        (x + dx) % RING, (y + sy) % RING, (z + sz) % RING, (core + dcore) % 2
                    )
                    pairs.append((place_of(x, y, z, core), to))
    return lax.ppermute(piece, ALL_AXES, pairs)


def around(piece, axis):
    return [piece] + [
        shift(piece, **{axis: RING - k}, swap_on_core_1=True) for k in range(1, RING)
    ]


def facing(x, second):
    odd = x % 2
    return (x + 3 + 2 * odd) % RING if second else x + 1 - 2 * odd


def trade(piece, later):
    pairs = [
        (place_of(x, y, z, core), place_of(facing(x, core != later), y, z, core))
        for x in range(RING)
        for y in range(RING)
        for z in range(RING)
        for core in range(2)
    ]
    return lax.ppermute(piece, ALL_AXES, pairs)


def gather(base, adapter_down_stack, adapter_up_stack, participant_weight):
    layers, ranks, cols = adapter_up_stack.shape
    up = adapter_up_stack.reshape(1, layers, ranks // 8, 8, cols)
    near_up = jnp.concatenate([up, trade(up, False)])
    far_up = trade(near_up, True)
    (here,) = stage([adapter_down_stack[None]])
    _, *others = around(adapter_down_stack[None], "dz")
    ring = jnp.concatenate([here, *others])
    mine, *others = around(ring, "dy")
    near_sorted, scale = sort_near(participant_weight, near_up)
    b_sorted = sort_far(far_up, near_sorted)
    touched = touch(base, [])
    others = [gate([piece], [touched, b_sorted])[0] for piece in others]
    own = [mine, *others]
    other = [shift(piece, dcore=1) for piece in own]
    return own + other, b_sorted, scale


def stage_kernel(*refs):
    half = len(refs) // 2
    for in_ref, out_ref in zip(refs[:half], refs[half:]):
        out_ref[...] = in_ref[...]


def stage(arrays):
    vmem = pl.BlockSpec(memory_space=pltpu.VMEM)
    return pl.pallas_call(
        stage_kernel,
        in_specs=[vmem] * len(arrays),
        out_specs=[vmem] * len(arrays),
        out_shape=[jax.ShapeDtypeStruct(a.shape, a.dtype) for a in arrays],
        compiler_params=pltpu.CompilerParams(vmem_limit_bytes=VMEM_LIMIT),
        cost_estimate=pl.CostEstimate(flops=0, bytes_accessed=1 << 20, transcendentals=0),
    )(*arrays)


def touch_kernel(base_ref, *refs):
    out_ref = refs[-1]
    out_ref[...] = jnp.zeros(out_ref.shape, out_ref.dtype)


def touch(base, after):
    anywhere, vmem = pl.BlockSpec(memory_space=pl.ANY), pl.BlockSpec(memory_space=pltpu.VMEM)
    return pl.pallas_call(
        touch_kernel,
        in_specs=[vmem] + [anywhere] * len(after),
        out_specs=vmem,
        out_shape=jax.ShapeDtypeStruct((8, 128), jnp.float32),
        compiler_params=pltpu.CompilerParams(vmem_limit_bytes=VMEM_LIMIT),
        cost_estimate=pl.CostEstimate(flops=0, bytes_accessed=4 * base.size, transcendentals=0),
    )(base, *after)


def gate(values, after):
    anywhere = pl.BlockSpec(memory_space=pl.ANY)
    specs = [anywhere] * len(values)
    return pl.pallas_call(
        lambda *refs: None,
        in_specs=specs + [anywhere] * len(after),
        out_specs=specs,
        out_shape=[jax.ShapeDtypeStruct(v.shape, v.dtype) for v in values],
        input_output_aliases={i: i for i in range(len(values))},
        compiler_params=pltpu.CompilerParams(vmem_limit_bytes=VMEM_LIMIT),
        cost_estimate=pl.CostEstimate(flops=0, bytes_accessed=0, transcendentals=0),
    )(*values, *after)


def place_blocks(b_ref, out_ref, far):
    row, col = lax.axis_index("row"), lax.axis_index("col")
    x, y, z, core = lax.axis_index("client"), col // 2, (col % 2) * 2 + row // 2, row % 2
    early, late = facing(x, False), facing(x, True)
    first_pair = jnp.where(core == 0, early, late)
    last_pair = jnp.where(core == 0, late, early)
    groups = (last_pair, lax.rem(x + 2, RING)) if far else (x, first_pair)
    for i, group in enumerate(groups):
        holder = lax.rem(group, 2)
        for block in range(8):
            dy = lax.rem(block // 2 - y + RING, RING)
            dz = lax.rem(block % 2 * 2 + group // 2 - z + RING, RING)
            first, second = jnp.where(holder == 0, dz, dy), jnp.where(holder == 0, dy, dz)
            slot = (lax.rem(holder + core, 2) * RING + second) * RING + first
            out_ref[:, slot] = b_ref[i, :, block]


def near_kernel(weight_ref, near_ref, out_ref, scale_ref):
    place_blocks(near_ref, out_ref, False)
    row, col = lax.axis_index("row"), lax.axis_index("col")
    y, z, core = col // 2, (col % 2) * 2 + row // 2, row % 2
    for dcore in range(2):
        holder = lax.rem(core + dcore, 2)
        for second in range(RING):
            for first in range(RING):
                dy = jnp.where(holder == 0, second, first)
                dz = jnp.where(holder == 0, first, second)
                y_from, z_from = lax.rem(y + dy, RING), lax.rem(z + dz, RING)
                client = (lax.rem(z_from, 2) * 2 + holder) * 4 + y_from
                scale_ref[(dcore * RING + second) * RING + first] = jnp.full(
                    scale_ref.shape[1:], weight_ref[client], jnp.float32
                )


def sort_near(participant_weight, near_up):
    _, layers, _, _, cols = near_up.shape
    vmem = pl.BlockSpec(memory_space=pltpu.VMEM)
    return pl.pallas_call(
        near_kernel,
        in_specs=[pl.BlockSpec(memory_space=pltpu.SMEM), vmem],
        out_specs=[vmem, vmem],
        out_shape=[
            jax.ShapeDtypeStruct((layers, BLOCKS, 8, cols), near_up.dtype),
            jax.ShapeDtypeStruct((BLOCKS, 8, 128), jnp.float32),
        ],
        compiler_params=pltpu.CompilerParams(vmem_limit_bytes=VMEM_LIMIT),
        cost_estimate=pl.CostEstimate(flops=0, bytes_accessed=4 * near_up.size, transcendentals=0),
    )(participant_weight, near_up)


def far_kernel(far_ref, _, out_ref):
    place_blocks(far_ref, out_ref, True)


def sort_far(far_up, near_sorted):
    vmem = pl.BlockSpec(memory_space=pltpu.VMEM)
    return pl.pallas_call(
        far_kernel,
        in_specs=[vmem, vmem],
        out_specs=vmem,
        out_shape=jax.ShapeDtypeStruct(near_sorted.shape, near_sorted.dtype),
        input_output_aliases={1: 0},
        compiler_params=pltpu.CompilerParams(vmem_limit_bytes=VMEM_LIMIT),
        cost_estimate=pl.CostEstimate(flops=0, bytes_accessed=4 * far_up.size, transcendentals=0),
    )(far_up, near_sorted)


def merge_kernel(base_ref, *refs):
    a_refs, (b_ref, scale_ref, out_ref) = refs[:-3], refs[-3:]
    layers, rows, cols = base_ref.shape
    part_rows = out_ref.shape[2]
    tall = 256
    per = tall // part_rows
    ranks = BLOCKS * 8
    scale = scale_ref[...].reshape(ranks, 128)
    scale = jnp.concatenate([scale] * (tall // 128), axis=1)
    rights = [b_ref[layer].reshape(ranks, cols) for layer in range(layers)]

    @pl.loop(0, rows // tall, unroll=8)
    def _(i):
        span = pl.ds(pl.multiple_of(i * tall, tall), tall)
        for layer in range(layers):
            left = jnp.concatenate(
                [ref[:, layer, :, span].reshape(-1, tall) for ref in a_refs]
            )
            left = (scale * left.astype(jnp.float32)).astype(jnp.bfloat16)
            delta = lax.dot_general(
                left, rights[layer], (((0,), (0,)), ((), ())), preferred_element_type=jnp.float32
            )
            merged = (base_ref[layer, span].astype(jnp.float32) + delta).astype(jnp.bfloat16)
            for part in range(per):
                place = i * per + part
                row, col = place // 8, lax.rem(place, 8)
                spot = spot_of(col // 2, lax.rem(col, 2) * 2 + row // 2, lax.rem(row, 2))
                out_ref[spot, layer] = merged[part * part_rows : (part + 1) * part_rows]


def merge(base, a_pieces, b_sorted, scale, parts):
    layers, rows, cols = base.shape
    vmem = pl.BlockSpec(memory_space=pltpu.VMEM)
    return pl.pallas_call(
        merge_kernel,
        in_specs=[vmem] * (len(a_pieces) + 3),
        out_specs=vmem,
        out_shape=jax.ShapeDtypeStruct((parts, layers, rows // parts, cols), jnp.bfloat16),
        compiler_params=pltpu.CompilerParams(vmem_limit_bytes=VMEM_LIMIT),
        cost_estimate=pl.CostEstimate(
            flops=2 * layers * rows * cols * 256, bytes_accessed=4 * base.size, transcendentals=0
        ),
    )(base, *a_pieces, b_sorted, scale)


def settle_kernel(in_ref, out_ref, lines, sems):
    _, layers, part_rows, cols = in_ref.shape
    tall = lines.shape[1]
    copies = []
    for layer in range(layers):
        for first in range(0, part_rows, tall):
            slot = len(copies)
            for y in range(RING):
                for z in range(RING):
                    for core in range(2):
                        left = place_of(0, y, z, core) * cols
                        lines[slot, :, left : left + cols] = in_ref[
                            spot_of(y, z, core), layer, first : first + tall
                        ]
            copies.append(
                pltpu.make_async_copy(
                    lines.at[slot], out_ref.at[layer, pl.ds(first, tall)], sems.at[slot]
                )
            )
            copies[-1].start()
    for copy in copies:
        copy.wait()


def settle(received):
    parts, layers, part_rows, cols = received.shape
    tall = 16
    slots = layers * part_rows // tall
    return pl.pallas_call(
        settle_kernel,
        in_specs=[pl.BlockSpec(memory_space=pltpu.VMEM)],
        out_specs=pl.BlockSpec(memory_space=pl.ANY),
        out_shape=jax.ShapeDtypeStruct((layers, part_rows, parts * cols), jnp.bfloat16),
        scratch_shapes=[
            pltpu.VMEM((slots, tall, parts * cols), jnp.bfloat16),
            pltpu.SemaphoreType.DMA((slots,)),
        ],
        compiler_params=pltpu.CompilerParams(vmem_limit_bytes=VMEM_LIMIT),
        cost_estimate=pl.CostEstimate(flops=0, bytes_accessed=4 * received.size, transcendentals=0),
    )(received)


def local(frozen_up_weight, adapter_down_stack, adapter_up_stack, participant_weight):
    parts = lax.axis_size(TILE_AXES)
    a_pieces, b_sorted, scale = gather(
        frozen_up_weight, adapter_down_stack, adapter_up_stack, participant_weight
    )
    merged = merge(frozen_up_weight, a_pieces, b_sorted, scale, parts)
    return settle(exchange(merged))


def solution(mesh):
    return jax.shard_map(
        local,
        mesh=mesh,
        in_specs=(
            P(None, "client", ("row", "col")),
            P(None, ("row", "col"), "client"),
            P(None, "client", ("row", "col")),
            P(),
        ),
        out_specs=P(None, ("client", "row", "col"), None),
        check_vma=False,
    )
```
